32 devices in a mesh: dp: 32 (over z, y, x, core).
Axes of the slice: x: 2, y: 2, z: 4, core: 2. Of those that a mesh axis runs over, the one named last changes fastest.
Arguments:
- tokens: bfloat16 [32768, 960], P('dp'), may hold values from -6 to 6
- position: int32 [32768], P('dp'), may hold values from -1 to 511, as said below
- cotangent: bfloat16 [32768, 960], P('dp'), may hold values from -6 to 6
- w_query: float32 [921600], P('dp'), may hold values from -0.1875 to 0.1875
- w_key: float32 [307200], P('dp'), may hold values from -0.1875 to 0.1875
- w_value: float32 [307200], P('dp'), may hold values from -0.1875 to 0.1875
- w_out: float32 [921600], P('dp'), may hold values from -1 to 1
- w_gate: float32 [2457600], P('dp'), may hold values from -0.1875 to 0.1875
- w_up: float32 [2457600], P('dp'), may hold values from -0.1875 to 0.1875
- w_down: float32 [2457600], P('dp'), may hold values from -0.125 to 0.125
- gain_attn: float32 [960], replicated, may hold values from 0.5 to 1.5
- gain_mlp: float32 [960], replicated, may hold values from 0.5 to 1.5
Outputs:
- output: bfloat16 [32768, 960], P('dp')
- grad_tokens: bfloat16 [32768, 960], P('dp')
- grad_w_query: float32 [921600], P('dp')
- grad_w_key: float32 [307200], P('dp')
- grad_w_value: float32 [307200], P('dp')
- grad_w_out: float32 [921600], P('dp')
- grad_w_gate: float32 [2457600], P('dp')
- grad_w_up: float32 [2457600], P('dp')
- grad_w_down: float32 [2457600], P('dp')
- grad_gain_attn: float32 [960], replicated
- grad_gain_mlp: float32 [960], replicated
The draws below stay inside these ranges and needn't reach their ends.
Inputs may be any that keep to these rules, and one draw needn't show every extreme that they name: `position`: within each aligned block of 512 slots (one micro-batch): slot 0 holds 0; every other live slot holds 0 (a new sequence) or one more than the slot before it; empty slots (-1) come only after the last live slot; a quarter or more of the slots are live; in every draw one micro-batch holds a single sequence of 512 tokens.
All inputs are finite; a program needn't handle non-finite values.
Results may differ from the reference program's by a relative error of at most 0.012.
The reference program's roundings to bfloat16 on the way count: a program that leaves them out, or rounds other values in their place, can miss the bound.
Values may be sent and summed in bfloat16 or wider, within the bound.
A program may use at most 320 MiB of HBM per device.

```python
import math
import jax
import jax.numpy as jnp
from jax import lax

D = 960
H = 15
KV = 5
HD = 64
FF = 2560
SLOTS = 512
TOKENS = 32768


def draw_position(key, part):
    key = jax.random.fold_in(key, 7)
    count_key, full_key, start_key = jax.random.split(key, 3)
    blocks = TOKENS // SLOTS
    live_count = SLOTS - jax.random.randint(count_key, (blocks,), 0, 3 * SLOTS // 4 + 1)
    chosen = jax.random.randint(full_key, (), 0, blocks)
    block_ids = jnp.arange(blocks, dtype=jnp.int32)
    live_count = jnp.where(block_ids == chosen, SLOTS, live_count)
    slot_ids = jnp.arange(SLOTS, dtype=jnp.int32)
    starts = jax.random.randint(start_key, (blocks, SLOTS), 0, max(SLOTS // 4, 2)) == 0
    starts = starts | (slot_ids[None, :] == 0)
    starts = starts & ((block_ids != chosen)[:, None] | (slot_ids[None, :] == 0))
    first = lax.cummax(jnp.where(starts, slot_ids[None, :], 0), axis=1)
    placed = slot_ids[None, :] - first
    placed = jnp.where(slot_ids[None, :] < live_count[:, None], placed, -1)
    return placed.reshape(TOKENS).astype(jnp.int32)


def block_scale(own_key, extent, pieces, low, largest):
    gain = 1.0
    for axis_at, parts in pieces:
        steps = jax.random.uniform(jax.random.fold_in(jax.random.fold_in(own_key, 6), axis_at), (parts,), jnp.float32, low / len(pieces), largest / len(pieces))
        gain = gain * jnp.repeat(jnp.exp(steps), extent[axis_at] // parts).reshape((-1,) + (1,) * (len(extent) - 1 - axis_at))
    return gain


def gaussian(own_key, shape, deviation, bound, cuts=(), kind=jnp.bfloat16):
    loudness = block_scale(own_key, shape, cuts, -0.22, 0.18) if cuts else 1.0
    array = jax.random.normal(own_key, shape, jnp.float32) * deviation * loudness
    return jnp.minimum(jnp.maximum(array, -bound), bound).astype(kind)


def setup_inputs(seed: int = 0) -> dict:
    seeds = jax.random.split(jax.random.key(seed), 13)
    return {
        "tokens": gaussian(seeds[0], (TOKENS, D), 1.0, 6.0, ((0, 32),)),
        "position": draw_position(jax.random.fold_in(seeds[12], 71), 0),
        "cotangent": gaussian(seeds[2], (TOKENS, D), 1.0, 6.0, ((0, 32),)),
        "w_query": gaussian(seeds[3], (D * D,), D ** -0.5, 0.1875, ((0, 32),), jnp.float32),
        "w_key": gaussian(seeds[4], (D * KV * HD,), D ** -0.5, 0.1875, ((0, 32),), jnp.float32),
        "w_value": gaussian(seeds[5], (D * KV * HD,), D ** -0.5, 0.1875, ((0, 32),), jnp.float32),
        "w_out": gaussian(seeds[6], (D * D,), (D // 32) ** -0.5, 1.0, ((0, 32),), jnp.float32),
        "w_gate": gaussian(seeds[7], (D * FF,), D ** -0.5, 0.1875, ((0, 32),), jnp.float32),
        "w_up": gaussian(seeds[8], (D * FF,), D ** -0.5, 0.1875, ((0, 32),), jnp.float32),
        "w_down": gaussian(seeds[9], (FF * D,), FF ** -0.5, 0.125, ((0, 32),), jnp.float32),
        "gain_attn": jnp.clip(1.0 + 0.1 * jax.random.normal(seeds[10], (D,), jnp.float32), 0.5, 1.5),
        "gain_mlp": jnp.clip(1.0 + 0.1 * jax.random.normal(seeds[11], (D,), jnp.float32), 0.5, 1.5),
    }


@jax.custom_vjp
def low(v):
    return lax.optimization_barrier(v.astype(jnp.bfloat16)).astype(jnp.float32)

@jax.custom_vjp
def low_back(v):
    return v

def low_keep(v):
    return (low(v), None)

def low_pass(kept, grad):
    return (grad,)

def back_keep(v):
    return (v, None)

def back_low(kept, grad):
    return (low(grad),)
low.defvjp(low_keep, low_pass)
low_back.defvjp(back_keep, back_low)
EPS = 1e-05
THETA = 100000.0
HIGH = lax.Precision.HIGHEST

def block_mask(position):
    living = position >= 0
    placed = jnp.maximum(position, 0)
    sequence = jnp.cumsum((position == 0).astype(jnp.int32))
    allowed = (sequence[:, None] == sequence[None, :]) & (placed[None, :] <= placed[:, None])
    allowed = allowed & living[:, None] & living[None, :]
    slot_ids = jnp.arange(position.shape[0])
    return (allowed | (slot_ids[:, None] == slot_ids[None, :]), placed, living)

def rotary_tables(placed, head_size):
    half_ids = jnp.arange(head_size // 2, dtype=jnp.float32)
    freqs = THETA ** (-2.0 * half_ids / head_size)
    angles = placed.astype(jnp.float32)[:, None] * freqs[None, :]
    return (jnp.cos(angles)[:, None, :], jnp.sin(angles)[:, None, :])

def rotate(values, cosines, sines):
    half = values.shape[-1] // 2
    first_half = values[..., :half]
    second_half = values[..., half:]
    return jnp.concatenate([first_half * cosines - second_half * sines, second_half * cosines + first_half * sines], axis=-1)

def layer(inputs, w_query, w_key, w_value, w_out, w_gate, w_up, w_down, gain_attn, gain_mlp, allowed, cosines, sines):
    rows = inputs.shape[0]
    groups = H // KV
    scale = 1.0 / math.sqrt(HD)
    factor_one = lax.rsqrt(lax.optimization_barrier(jnp.mean(inputs * inputs, axis=-1, keepdims=True)) + EPS)
    normed = low(inputs * factor_one * gain_attn)
    query = low_back(jnp.dot(normed, low(w_query), precision=HIGH)).reshape(rows, H, HD)
    keys = low_back(jnp.dot(normed, low(w_key), precision=HIGH)).reshape(rows, KV, HD)
    values = low(low_back(jnp.dot(normed, low(w_value), precision=HIGH))).reshape(rows, KV, HD)
    query_rot = low(rotate(query, cosines, sines)).reshape(rows, KV, groups, HD)
    keys_rot = low(rotate(keys, cosines, sines))
    scores = low_back(jnp.einsum('sgrd,tgd->grst', query_rot, keys_rot, precision=HIGH) * scale)
    scores = jnp.where(allowed, scores, -1e+30)
    top = lax.optimization_barrier(jnp.max(scores, axis=-1, keepdims=True))
    expd = jnp.exp(scores - top)
    probs = expd / lax.optimization_barrier(jnp.sum(expd, axis=-1, keepdims=True))
    mixed = jnp.einsum('grst,tgd->sgrd', low(probs), values, precision=HIGH).reshape(rows, D)
    mixed = low_back(low(mixed))
    resid = inputs + low_back(jnp.dot(mixed, low(w_out), precision=HIGH))
    factor_two = lax.rsqrt(lax.optimization_barrier(jnp.mean(resid * resid, axis=-1, keepdims=True)) + EPS)
    normed_two = low(resid * factor_two * gain_mlp)
    gate = low_back(jnp.dot(normed_two, low(w_gate), precision=HIGH))
    upper = low_back(jnp.dot(normed_two, low(w_up), precision=HIGH))
    hidden = low(gate * jax.nn.sigmoid(gate) * upper)
    branch = low_back(jnp.dot(hidden, low(w_down), precision=HIGH))
    return resid + branch

def reference(tokens, position, cotangent, w_query, w_key, w_value, w_out, w_gate, w_up, w_down, gain_attn, gain_mlp):
    blocks = TOKENS // SLOTS
    params = (w_query.reshape(D, D), w_key.reshape(D, KV * HD), w_value.reshape(D, KV * HD), w_out.reshape(D, D), w_gate.reshape(D, FF), w_up.reshape(D, FF), w_down.reshape(FF, D), gain_attn, gain_mlp)
    items = (tokens.reshape(blocks, SLOTS, D), position.reshape(blocks, SLOTS), cotangent.reshape(blocks, SLOTS, D))

    def one_block(totals, item):
        block_tokens, block_pos, block_cot = item
        allowed, placed, living = block_mask(block_pos)
        cosines, sines = rotary_tables(placed, HD)

        def forward(inputs, *weights):
            return layer(inputs, *weights, allowed, cosines, sines)
        result, pull = jax.vjp(forward, block_tokens.astype(jnp.float32), *params)
        grads = pull(block_cot.astype(jnp.float32) * living[:, None].astype(jnp.float32))
        new_totals = tuple((total + grad for total, grad in zip(totals, grads[1:])))
        return (new_totals, (result.astype(jnp.bfloat16), grads[0].astype(jnp.bfloat16)))
    start = tuple((jnp.zeros_like(param) for param in params))
    totals, (results, input_grads) = lax.scan(one_block, start, items)
    return (results.reshape(TOKENS, D), input_grads.reshape(TOKENS, D), totals[0].reshape(-1), totals[1].reshape(-1), totals[2].reshape(-1), totals[3].reshape(-1), totals[4].reshape(-1), totals[5].reshape(-1), totals[6].reshape(-1), totals[7], totals[8])
```

```python
import math

import jax
import jax.numpy as jnp
from jax import lax
from jax.sharding import PartitionSpec as P

D = 960
H = 15
KV = 5
HD = 64
FF = 2560
SLOTS = 512


EPS = 1e-05
THETA = 100000.0


def block_mask(position):
    living = position >= 0
    placed = jnp.maximum(position, 0)
    sequence = jnp.cumsum((position == 0).astype(jnp.int32))
    allowed = (sequence[:, None] == sequence[None, :]) & (placed[None, :] <= placed[:, None])
    allowed = allowed & living[:, None] & living[None, :]
    slot_ids = jnp.arange(position.shape[0])
    return (allowed | (slot_ids[:, None] == slot_ids[None, :]), placed, living)


def rotary_tables(placed, head_size):
    half_ids = jnp.arange(head_size // 2, dtype=jnp.float32)
    freqs = THETA ** (-2.0 * half_ids / head_size)
    angles = placed.astype(jnp.float32)[:, None] * freqs[None, :]
    return (jnp.cos(angles)[:, None, :], jnp.sin(angles)[:, None, :])


def rotate(values, cosines, sines):
    half = values.shape[-1] // 2
    first_half = values[..., :half]
    second_half = values[..., half:]
    return jnp.concatenate(
        [first_half * cosines - second_half * sines, second_half * cosines + first_half * sines],
        axis=-1,
    )


def unrotate(grads, cosines, sines):
    half = grads.shape[-1] // 2
    first_half = grads[..., :half]
    second_half = grads[..., half:]
    return jnp.concatenate(
        [first_half * cosines + second_half * sines, second_half * cosines - first_half * sines],
        axis=-1,
    )


def matmul(first, second):
    return jnp.dot(first, second, preferred_element_type=jnp.float32)


def left_contract(first, second):
    return lax.dot_general(
        first, second, (((0,), (0,)), ((), ())), preferred_element_type=jnp.float32
    )


def right_contract(first, second):
    return lax.dot_general(
        first, second, (((1,), (1,)), ((), ())), preferred_element_type=jnp.float32
    )


def norm_back(grad_out, inputs, factor, gain):
    scaled = grad_out * gain
    return factor * scaled - inputs * factor * factor * factor * jnp.mean(
        scaled * inputs, axis=-1, keepdims=True
    )


def swap(value, bit):
    owners = lax.axis_size("dp")
    return lax.ppermute(value, "dp", [(i, i ^ (1 << bit)) for i in range(owners)])


def my_bit(bit):
    return (lax.axis_index("dp") >> bit) & 1


def gather_rows(shard, order):
    current = shard[None]
    held = []
    for bit in order:
        other = swap(current, bit)
        place = sum(1 for b in held if b > bit)
        shape = current.shape
        split = (1 << place, 1, shape[0] >> place) + shape[1:]
        mine, theirs = current.reshape(split), other.reshape(split)
        upper = my_bit(bit) == 1
        low = jnp.where(upper, theirs, mine)
        high = jnp.where(upper, mine, theirs)
        current = jnp.concatenate([low, high], axis=1).reshape((shape[0] * 2,) + shape[1:])
        held.append(bit)
    return current


def scatter_rows(parts, order):
    current = parts
    left = list(range(len(order)))
    for step, bit in enumerate(order):
        place = sum(1 for b in left if b > bit)
        shape = current.shape
        split = (1 << place, 2, shape[0] >> (place + 1)) + shape[1:]
        view = current.reshape(split)
        mine = my_bit(bit)
        sent = lax.dynamic_index_in_dim(view, 1 - mine, 1, keepdims=False)
        kept = lax.dynamic_index_in_dim(view, mine, 1, keepdims=False)
        got = swap(sent, bit)
        total = kept.astype(jnp.float32) + got.astype(jnp.float32)
        if step < len(order) - 1:
            total = total.astype(jnp.bfloat16)
        current = total.reshape((shape[0] // 2,) + shape[1:])
        left.remove(bit)
    return current[0]


def total_over(value, order):
    for bit in order:
        value = value + swap(value, bit)
    return value


def orders():
    bits = max(lax.axis_size("dp").bit_length() - 1, 0)
    far = list(range(3, bits))
    near_x = [bit for bit in (1, 2) if bit < bits]
    core = [0] if bits else []
    return core, near_x, far


def gather_order(flip):
    core, near, far = orders()
    return far + (near[::-1] if flip else near) + core


def scatter_order(flip):
    core, near, far = orders()
    return core + (near[::-1] if flip else near) + far[::-1]


def whole_rows(flat, width):
    return flat.shape[0] % width == 0


def gather_matrix(flat, width, flip):
    shard = flat.astype(jnp.bfloat16)
    if whole_rows(flat, width):
        shard = flat.reshape(-1, width).astype(jnp.bfloat16)
    return gather_rows(shard, gather_order(flip)).reshape(-1, width)


def scatter_matrix(grad, flip):
    owners = lax.axis_size("dp")
    grad = grad.astype(jnp.bfloat16)
    if grad.shape[0] % owners == 0:
        parts = grad.reshape(owners, grad.shape[0] // owners, grad.shape[1])
    else:
        parts = grad.reshape(owners, -1)
    return scatter_rows(parts, scatter_order(flip))


def attend(query_rot, keys_rot, values, allowed, scale):
    scores = (
        jnp.einsum("bsgrd,btgd->bgrst", query_rot, keys_rot, preferred_element_type=jnp.float32)
        * scale
    )
    return jnp.where(allowed[:, None, None], scores, -1e30)


def body(
    tokens,
    position,
    cotangent,
    w_query,
    w_key,
    w_value,
    w_out,
    w_gate,
    w_up,
    w_down,
    gain_attn,
    gain_mlp,
):
    slots = SLOTS
    groups = H // KV
    kvw = KV * HD
    scale = 1.0 / math.sqrt(HD)
    rows = tokens.shape[0]
    blocks = rows // slots
    if whole_rows(w_query, D):
        joined = jnp.concatenate(
            [
                w_query.reshape(-1, D),
                w_key.reshape(-1, kvw),
                w_value.reshape(-1, kvw),
                w_out.reshape(-1, D),
            ],
            axis=1,
        ).astype(jnp.bfloat16)
        joined = gather_rows(joined, gather_order(False)).reshape(D, D + 2 * kvw + D)
        mat_qkv = joined[:, : D + 2 * kvw]
        mat_out = joined[:, D + 2 * kvw :]
    else:
        mat_qkv = jnp.concatenate(
            [
                gather_matrix(w_query, D, False),
                gather_matrix(w_key, kvw, False),
                gather_matrix(w_value, kvw, False),
            ],
            axis=1,
        )
        mat_out = gather_matrix(w_out, D, False)
    mat_gate = gather_matrix(w_gate, FF, True)
    mat_up = gather_matrix(w_up, FF, False)
    mat_down = gather_matrix(w_down, D, True)

    allowed, placed, living = jax.vmap(block_mask)(position.reshape(blocks, slots))
    cosines, sines = rotary_tables(placed.reshape(-1), HD)
    living = living.reshape(-1)
    inputs = tokens.astype(jnp.float32)
    factor_one = lax.rsqrt(jnp.mean(inputs * inputs, axis=-1, keepdims=True) + EPS)
    normed = (inputs * factor_one * gain_attn).astype(jnp.bfloat16)
    qkv = matmul(normed, mat_qkv)
    query = qkv[:, :D].reshape(rows, H, HD)
    keys = qkv[:, D : D + kvw].reshape(rows, KV, HD)
    values = qkv[:, D + kvw :].astype(jnp.bfloat16).reshape(blocks, slots, KV, HD)
    query_rot = (
        rotate(query, cosines, sines).astype(jnp.bfloat16).reshape(blocks, slots, KV, groups, HD)
    )
    keys_rot = rotate(keys, cosines, sines).astype(jnp.bfloat16).reshape(blocks, slots, KV, HD)
    scores = attend(query_rot, keys_rot, values, allowed, scale)
    top = jnp.max(scores, axis=-1, keepdims=True)
    expd = jnp.exp(scores - top)
    total_exp = jnp.sum(expd, axis=-1, keepdims=True)
    probs = (expd / total_exp).astype(jnp.bfloat16)
    mixed = jnp.einsum("bgrst,btgd->bsgrd", probs, values, preferred_element_type=jnp.float32)
    mixed = mixed.reshape(rows, D).astype(jnp.bfloat16)
    resid = inputs + matmul(mixed, mat_out)
    factor_two = lax.rsqrt(jnp.mean(resid * resid, axis=-1, keepdims=True) + EPS)
    normed_two = (resid * factor_two * gain_mlp).astype(jnp.bfloat16)
    gate = matmul(normed_two, mat_gate)
    upper = matmul(normed_two, mat_up)
    sigma = jax.nn.sigmoid(gate)
    hidden = (gate * sigma * upper).astype(jnp.bfloat16)
    result = (resid + matmul(hidden, mat_down)).astype(jnp.bfloat16)

    grad_out = cotangent.astype(jnp.float32) * living[:, None].astype(jnp.float32)
    grad_out_b = grad_out.astype(jnp.bfloat16)
    sum_down = scatter_matrix(left_contract(hidden, grad_out_b), False)
    d_hidden = right_contract(grad_out_b, mat_down)
    d_upper = (d_hidden * gate * sigma).astype(jnp.bfloat16)
    d_gate = (d_hidden * upper * sigma * (1.0 + gate * (1.0 - sigma))).astype(jnp.bfloat16)
    sum_gate = scatter_matrix(left_contract(normed_two, d_gate), True)
    sum_up = scatter_matrix(left_contract(normed_two, d_upper), False)
    d_normed_two = right_contract(d_gate, mat_gate) + right_contract(d_upper, mat_up)
    gain_two = jnp.sum(d_normed_two * resid * factor_two, axis=0)
    d_resid = grad_out + norm_back(d_normed_two, resid, factor_two, gain_mlp)
    d_attn = d_resid.astype(jnp.bfloat16)
    sum_wout = scatter_matrix(left_contract(mixed, d_attn), True)
    d_mixed = right_contract(d_attn, mat_out).astype(jnp.bfloat16)
    d_mixed = d_mixed.reshape(blocks, slots, KV, groups, HD)
    d_probs = jnp.einsum("bsgrd,btgd->bgrst", d_mixed, values, preferred_element_type=jnp.float32)
    probs_back = expd / total_exp
    d_values = jnp.einsum("bgrst,bsgrd->btgd", probs, d_mixed, preferred_element_type=jnp.float32)
    d_values = d_values.reshape(rows, kvw).astype(jnp.bfloat16)
    d_scores = probs_back * (d_probs - jnp.sum(probs_back * d_probs, axis=-1, keepdims=True))
    d_scores = d_scores.astype(jnp.bfloat16)
    d_query_rot = (
        jnp.einsum("bgrst,btgd->bsgrd", d_scores, keys_rot, preferred_element_type=jnp.float32)
        * scale
    )
    d_keys_rot = (
        jnp.einsum("bgrst,bsgrd->btgd", d_scores, query_rot, preferred_element_type=jnp.float32)
        * scale
    )
    d_query = unrotate(d_query_rot.reshape(rows, H, HD), cosines, sines).reshape(rows, D)
    d_keys = unrotate(d_keys_rot.reshape(rows, KV, HD), cosines, sines).reshape(rows, kvw)
    d_qkv = jnp.concatenate(
        [d_query.astype(jnp.bfloat16), d_keys.astype(jnp.bfloat16), d_values], axis=1
    )
    grad_qkv = left_contract(normed, d_qkv)
    if whole_rows(w_query, D):
        sum_qkv = scatter_matrix(grad_qkv, False)
        sum_query = sum_qkv[:, :D]
        sum_key = sum_qkv[:, D : D + kvw]
        sum_value = sum_qkv[:, D + kvw :]
    else:
        sum_query = scatter_matrix(grad_qkv[:, :D], False)
        sum_key = scatter_matrix(grad_qkv[:, D : D + kvw], False)
        sum_value = scatter_matrix(grad_qkv[:, D + kvw :], False)
    d_normed = right_contract(d_qkv, mat_qkv)
    gain_one = jnp.sum(d_normed * inputs * factor_one, axis=0)
    d_inputs = (d_resid + norm_back(d_normed, inputs, factor_one, gain_attn)).astype(jnp.bfloat16)
    gains = total_over(jnp.stack([gain_one, gain_two]), scatter_order(True))
    return (
        result,
        d_inputs,
        sum_query.reshape(-1),
        sum_key.reshape(-1),
        sum_value.reshape(-1),
        sum_wout.reshape(-1),
        sum_gate.reshape(-1),
        sum_up.reshape(-1),
        sum_down.reshape(-1),
        gains[0],
        gains[1],
    )


def solution(mesh):
    placed = (
        P("dp", None),
        P("dp"),
        P("dp", None),
        P("dp"),
        P("dp"),
        P("dp"),
        P("dp"),
        P("dp"),
        P("dp"),
        P("dp"),
        P(),
        P(),
    )
    return jax.shard_map(
        body,
        mesh=mesh,
        in_specs=placed,
        out_specs=(
            P("dp", None),
            P("dp", None),
            P("dp"),
            P("dp"),
            P("dp"),
            P("dp"),
            P("dp"),
            P("dp"),
            P("dp"),
            P(),
            P(),
        ),
        check_vma=False,
    )
```

```python
import math

import jax
import jax.numpy as jnp
from jax import lax
from jax.sharding import PartitionSpec as P

D = 960
H = 15
KV = 5
HD = 64
FF = 2560
SLOTS = 512


EPS = 1e-05
THETA = 100000.0


def block_mask(position):
    living = position >= 0
    placed = jnp.maximum(position, 0)
    sequence = jnp.cumsum((position == 0).astype(jnp.int32))
    allowed = (sequence[:, None] == sequence[None, :]) & (placed[None, :] <= placed[:, None])
    allowed = allowed & living[:, None] & living[None, :]
    slot_ids = jnp.arange(position.shape[0])
    return (allowed | (slot_ids[:, None] == slot_ids[None, :]), placed, living)


def rotary_tables(placed, head_size):
    half_ids = jnp.arange(head_size // 2, dtype=jnp.float32)
    freqs = THETA ** (-2.0 * half_ids / head_size)
    angles = placed.astype(jnp.float32)[:, None] * freqs[None, :]
    return (jnp.cos(angles)[:, None, :], jnp.sin(angles)[:, None, :])


def rotate(values, cosines, sines):
    half = values.shape[-1] // 2
    first_half = values[..., :half]
    second_half = values[..., half:]
    return jnp.concatenate(
        [first_half * cosines - second_half * sines, second_half * cosines + first_half * sines],
        axis=-1,
    )


def unrotate(grads, cosines, sines):
    half = grads.shape[-1] // 2
    first_half = grads[..., :half]
    second_half = grads[..., half:]
    return jnp.concatenate(
        [first_half * cosines + second_half * sines, second_half * cosines - first_half * sines],
        axis=-1,
    )


def matmul(first, second):
    return jnp.dot(first, second, preferred_element_type=jnp.float32)


def left_contract(first, second):
    return lax.dot_general(
        first, second, (((0,), (0,)), ((), ())), preferred_element_type=jnp.float32
    )


def right_contract(first, second):
    return lax.dot_general(
        first, second, (((1,), (1,)), ((), ())), preferred_element_type=jnp.float32
    )


def norm_back(grad_out, inputs, factor, gain):
    scaled = grad_out * gain
    return factor * scaled - inputs * factor * factor * factor * jnp.mean(
        scaled * inputs, axis=-1, keepdims=True
    )


def swap(value, bit):
    owners = lax.axis_size("dp")
    return lax.ppermute(value, "dp", [(i, i ^ (1 << bit)) for i in range(owners)])


def my_bit(bit):
    return (lax.axis_index("dp") >> bit) & 1


def gather_rows(shard, order):
    current = shard[None]
    held = []
    for bit in order:
        other = swap(current, bit)
        place = sum(1 for b in held if b > bit)
        shape = current.shape
        split = (1 << place, 1, shape[0] >> place) + shape[1:]
        mine, theirs = current.reshape(split), other.reshape(split)
        upper = my_bit(bit) == 1
        low = jnp.where(upper, theirs, mine)
        high = jnp.where(upper, mine, theirs)
        current = jnp.concatenate([low, high], axis=1).reshape((shape[0] * 2,) + shape[1:])
        held.append(bit)
    return current


class Halving:
    def __init__(self, parts, order):
        self.current = parts
        self.order = list(order)
        self.left = sorted(order)

    def step(self):
        if not self.order:
            return
        bit = self.order.pop(0)
        place = sum(1 for b in self.left if b > bit)
        shape = self.current.shape
        view = self.current.reshape((1 << place, 2, shape[0] >> (place + 1)) + shape[1:])
        mine = my_bit(bit)
        sent = lax.dynamic_index_in_dim(view, 1 - mine, 1, keepdims=False)
        kept = lax.dynamic_index_in_dim(view, mine, 1, keepdims=False)
        got = swap(sent, bit)
        total = kept.astype(jnp.float32) + got.astype(jnp.float32)
        if self.order:
            total = total.astype(jnp.bfloat16)
        self.current = total.reshape((shape[0] // 2,) + shape[1:])
        self.left.remove(bit)

    def finish(self):
        while self.order:
            self.step()
        return self.current[0]


def advance(chains, *values):
    held, values = lax.optimization_barrier((tuple(c.current for c in chains), values))
    for chain, current in zip(chains, held):
        chain.current = current
        chain.step()
    return values if len(values) > 1 else values[0]


def total_over(value, order):
    for bit in order:
        value = value + swap(value, bit)
    return value


def orders():
    bits = max(lax.axis_size("dp").bit_length() - 1, 0)
    far = list(range(3, bits))
    near_x = [bit for bit in (1, 2) if bit < bits]
    core = [0] if bits else []
    return core, near_x, far


def gather_order(flip):
    core, near, far = orders()
    return far + (near[::-1] if flip else near) + core


def scatter_order(flip):
    core, near, far = orders()
    return core + (near[::-1] if flip else near) + far[::-1]


def padded(height):
    return -(-height // 16) * 16


def spread(height, owners):
    pad = padded(height)
    row = lax.broadcasted_iota(jnp.int32, (height * owners, owners * pad), 0)
    column = lax.broadcasted_iota(jnp.int32, (height * owners, owners * pad), 1)
    inner = column % pad
    hit = (inner < height) & (row == column // pad * height + inner)
    return hit.astype(jnp.bfloat16)


def gather_padded(shard, chosen, flip):
    height = shard.shape[0]
    shard = jnp.pad(shard.astype(jnp.bfloat16), ((0, padded(height) - height), (0, 0)))
    full = gather_rows(shard, gather_order(flip))
    return matmul(chosen, full.reshape(-1, shard.shape[1])).astype(jnp.bfloat16)


def whole_rows(flat, width):
    return flat.shape[0] % width == 0


def gather_matrix(flat, width, flip):
    shard = flat.astype(jnp.bfloat16)
    if whole_rows(flat, width):
        shard = flat.reshape(-1, width).astype(jnp.bfloat16)
    return gather_rows(shard, gather_order(flip)).reshape(-1, width)


def scatter_matrix(grad, flip):
    owners = lax.axis_size("dp")
    grad = grad.astype(jnp.bfloat16)
    if grad.shape[0] % owners == 0:
        parts = grad.reshape(owners, grad.shape[0] // owners, grad.shape[1])
    else:
        parts = grad.reshape(owners, -1)
    return Halving(parts, scatter_order(flip))


def attend(query_rot, keys_rot, values, allowed, scale):
    scores = (
        jnp.einsum("bsgrd,btgd->bgrst", query_rot, keys_rot, preferred_element_type=jnp.float32)
        * scale
    )
    return jnp.where(allowed[:, None, None], scores, -1e30)


def body(
    tokens,
    position,
    cotangent,
    w_query,
    w_key,
    w_value,
    w_out,
    w_gate,
    w_up,
    w_down,
    gain_attn,
    gain_mlp,
):
    slots = SLOTS
    groups = H // KV
    kvw = KV * HD
    scale = 1.0 / math.sqrt(HD)
    rows = tokens.shape[0]
    blocks = rows // slots
    height = w_query.shape[0] // D
    aligned = whole_rows(w_query, D)
    if aligned:
        chosen = spread(height, lax.axis_size("dp"))
        joined = jnp.concatenate(
            [
                w_query.reshape(-1, D),
                w_key.reshape(-1, kvw),
                w_value.reshape(-1, kvw),
                w_out.reshape(-1, D),
            ],
            axis=1,
        )
        joined = gather_padded(joined, chosen, False)
        mat_qkv = joined[:, : D + 2 * kvw]
        mat_out = joined[:, D + 2 * kvw :]
    else:
        mat_qkv = jnp.concatenate(
            [
                gather_matrix(w_query, D, False),
                gather_matrix(w_key, kvw, False),
                gather_matrix(w_value, kvw, False),
            ],
            axis=1,
        )
        mat_out = gather_matrix(w_out, D, False)
    if aligned:
        mat_gate = gather_padded(w_gate.reshape(-1, FF), chosen, True)
        mat_up = gather_padded(w_up.reshape(-1, FF), chosen, False)
    else:
        mat_gate = gather_matrix(w_gate, FF, True)
        mat_up = gather_matrix(w_up, FF, False)

    def widen(value):
        return matmul(value, chosen).astype(jnp.bfloat16) if aligned else value

    mat_down = gather_matrix(w_down, D, True)

    allowed, placed, living = jax.vmap(block_mask)(position.reshape(blocks, slots))
    cosines, sines = rotary_tables(placed.reshape(-1), HD)
    living = living.reshape(-1)
    inputs = tokens.astype(jnp.float32)
    factor_one = lax.rsqrt(jnp.mean(inputs * inputs, axis=-1, keepdims=True) + EPS)
    normed = (inputs * factor_one * gain_attn).astype(jnp.bfloat16)
    qkv = matmul(normed, mat_qkv)
    query = qkv[:, :D].reshape(rows, H, HD)
    keys = qkv[:, D : D + kvw].reshape(rows, KV, HD)
    values = qkv[:, D + kvw :].astype(jnp.bfloat16).reshape(blocks, slots, KV, HD)
    query_rot = (
        rotate(query, cosines, sines).astype(jnp.bfloat16).reshape(blocks, slots, KV, groups, HD)
    )
    keys_rot = rotate(keys, cosines, sines).astype(jnp.bfloat16).reshape(blocks, slots, KV, HD)
    scores = attend(query_rot, keys_rot, values, allowed, scale)
    top = jnp.max(scores, axis=-1, keepdims=True)
    expd = jnp.exp(scores - top)
    total_exp = jnp.sum(expd, axis=-1, keepdims=True)
    probs = (expd / total_exp).astype(jnp.bfloat16)
    mixed = jnp.einsum("bgrst,btgd->bsgrd", probs, values, preferred_element_type=jnp.float32)
    mixed = mixed.reshape(rows, D).astype(jnp.bfloat16)
    resid = inputs + matmul(mixed, mat_out)
    factor_two = lax.rsqrt(jnp.mean(resid * resid, axis=-1, keepdims=True) + EPS)
    normed_two = (resid * factor_two * gain_mlp).astype(jnp.bfloat16)
    wide_two = widen(normed_two)
    gate = matmul(normed_two, mat_gate)
    upper = matmul(normed_two, mat_up)
    sigma = jax.nn.sigmoid(gate)
    hidden = (gate * sigma * upper).astype(jnp.bfloat16)
    result = (resid + matmul(hidden, mat_down)).astype(jnp.bfloat16)

    grad_out = cotangent.astype(jnp.float32) * living[:, None].astype(jnp.float32)
    grad_out_b = grad_out.astype(jnp.bfloat16)
    down = scatter_matrix(left_contract(hidden, grad_out_b), False)
    grad_out_b = advance([down], grad_out_b)
    d_hidden = right_contract(grad_out_b, mat_down)
    d_upper = (d_hidden * gate * sigma).astype(jnp.bfloat16)
    d_gate = (d_hidden * upper * sigma * (1.0 + gate * (1.0 - sigma))).astype(jnp.bfloat16)
    d_upper, d_gate = advance([down], d_upper, d_gate)
    gated = scatter_matrix(left_contract(wide_two, d_gate), True)
    raised = scatter_matrix(left_contract(wide_two, d_upper), False)
    d_upper, d_gate = advance([gated, raised, down], d_upper, d_gate)
    d_normed_two = right_contract(d_gate, mat_gate) + right_contract(d_upper, mat_up)
    gain_two = jnp.sum(d_normed_two * resid * factor_two, axis=0)
    d_resid = grad_out + norm_back(d_normed_two, resid, factor_two, gain_mlp)
    d_attn = d_resid.astype(jnp.bfloat16)
    d_attn = advance([gated], d_attn)
    wout = scatter_matrix(left_contract(widen(mixed), d_attn), True)
    d_mixed = right_contract(d_attn, mat_out).astype(jnp.bfloat16)
    d_mixed = d_mixed.reshape(blocks, slots, KV, groups, HD)
    d_mixed = advance([wout, raised, down], d_mixed)
    d_probs = jnp.einsum("bsgrd,btgd->bgrst", d_mixed, values, preferred_element_type=jnp.float32)
    probs_back = expd / total_exp
    d_values = jnp.einsum("bgrst,bsgrd->btgd", probs, d_mixed, preferred_element_type=jnp.float32)
    d_values = d_values.reshape(rows, kvw).astype(jnp.bfloat16)
    d_scores = probs_back * (d_probs - jnp.sum(probs_back * d_probs, axis=-1, keepdims=True))
    d_scores = d_scores.astype(jnp.bfloat16)
    d_scores = advance([wout, gated, raised, down], d_scores)
    d_query_rot = (
        jnp.einsum("bgrst,btgd->bsgrd", d_scores, keys_rot, preferred_element_type=jnp.float32)
        * scale
    )
    d_keys_rot = (
        jnp.einsum("bgrst,bsgrd->btgd", d_scores, query_rot, preferred_element_type=jnp.float32)
        * scale
    )
    d_query_rot, d_keys_rot = advance([wout, gated, raised], d_query_rot, d_keys_rot)
    d_query = unrotate(d_query_rot.reshape(rows, H, HD), cosines, sines).reshape(rows, D)
    d_keys = unrotate(d_keys_rot.reshape(rows, KV, HD), cosines, sines).reshape(rows, kvw)
    d_qkv = jnp.concatenate(
        [d_query.astype(jnp.bfloat16), d_keys.astype(jnp.bfloat16), d_values], axis=1
    )
    d_qkv = advance([wout, gated, raised], d_qkv)
    grad_qkv = left_contract(widen(normed), d_qkv)
    if aligned:
        joint = scatter_matrix(grad_qkv, False)
        d_qkv = advance([joint, wout], d_qkv)
    d_normed = right_contract(d_qkv, mat_qkv)
    gain_one = jnp.sum(d_normed * inputs * factor_one, axis=0)
    d_inputs = (d_resid + norm_back(d_normed, inputs, factor_one, gain_attn)).astype(jnp.bfloat16)
    gains = total_over(jnp.stack([gain_one, gain_two]), scatter_order(True))
    if aligned:
        sum_qkv = joint.finish()[:height]
        sum_query = sum_qkv[:, :D]
        sum_key = sum_qkv[:, D : D + kvw]
        sum_value = sum_qkv[:, D + kvw :]
        sum_wout, sum_gate, sum_up = [c.finish()[:height] for c in (wout, gated, raised)]
    else:
        sum_query = scatter_matrix(grad_qkv[:, :D], False).finish()
        sum_key = scatter_matrix(grad_qkv[:, D : D + kvw], False).finish()
        sum_value = scatter_matrix(grad_qkv[:, D + kvw :], False).finish()
        sum_wout, sum_gate, sum_up = wout.finish(), gated.finish(), raised.finish()
    sum_down = down.finish()
    return (
        result,
        d_inputs,
        sum_query.reshape(-1),
        sum_key.reshape(-1),
        sum_value.reshape(-1),
        sum_wout.reshape(-1),
        sum_gate.reshape(-1),
        sum_up.reshape(-1),
        sum_down.reshape(-1),
        gains[0],
        gains[1],
    )


def solution(mesh):
    placed = (
        P("dp", None),
        P("dp"),
        P("dp", None),
        P("dp"),
        P("dp"),
        P("dp"),
        P("dp"),
        P("dp"),
        P("dp"),
        P("dp"),
        P(),
        P(),
    )
    return jax.shard_map(
        body,
        mesh=mesh,
        in_specs=placed,
        out_specs=(
            P("dp", None),
            P("dp", None),
            P("dp"),
            P("dp"),
            P("dp"),
            P("dp"),
            P("dp"),
            P("dp"),
            P("dp"),
            P(),
            P(),
        ),
        check_vma=False,
    )
```

```python
import math

import jax
import jax.numpy as jnp
from jax import lax
from jax.sharding import PartitionSpec as P

D = 960
H = 15
KV = 5
HD = 64
FF = 2560
SLOTS = 512


EPS = 1e-05
THETA = 100000.0


def block_mask(position):
    living = position >= 0
    placed = jnp.maximum(position, 0)
    sequence = jnp.cumsum((position == 0).astype(jnp.int32))
    allowed = (sequence[:, None] == sequence[None, :]) & (placed[None, :] <= placed[:, None])
    allowed = allowed & living[:, None] & living[None, :]
    slot_ids = jnp.arange(position.shape[0])
    return (allowed | (slot_ids[:, None] == slot_ids[None, :]), placed, living)


def rotary_tables(placed, head_size):
    half_ids = jnp.arange(head_size // 2, dtype=jnp.float32)
    freqs = THETA ** (-2.0 * half_ids / head_size)
    angles = placed.astype(jnp.float32)[:, None] * freqs[None, :]
    return (jnp.cos(angles)[:, None, :], jnp.sin(angles)[:, None, :])


def rotate(values, cosines, sines):
    half = values.shape[-1] // 2
    first_half = values[..., :half]
    second_half = values[..., half:]
    return jnp.concatenate(
        [first_half * cosines - second_half * sines, second_half * cosines + first_half * sines],
        axis=-1,
    )


def unrotate(grads, cosines, sines):
    half = grads.shape[-1] // 2
    first_half = grads[..., :half]
    second_half = grads[..., half:]
    return jnp.concatenate(
        [first_half * cosines + second_half * sines, second_half * cosines - first_half * sines],
        axis=-1,
    )


def matmul(first, second):
    return jnp.dot(first, second, preferred_element_type=jnp.float32)


def left_contract(first, second):
    return lax.dot_general(
        first, second, (((0,), (0,)), ((), ())), preferred_element_type=jnp.float32
    )


def right_contract(first, second):
    return lax.dot_general(
        first, second, (((1,), (1,)), ((), ())), preferred_element_type=jnp.float32
    )


def norm_back(grad_out, inputs, factor, gain):
    scaled = grad_out * gain
    return factor * scaled - inputs * factor * factor * factor * jnp.mean(
        scaled * inputs, axis=-1, keepdims=True
    )


def swap(value, bit):
    owners = lax.axis_size("dp")
    return lax.ppermute(value, "dp", [(i, i ^ (1 << bit)) for i in range(owners)])


def my_bit(bit):
    return (lax.axis_index("dp") >> bit) & 1


class Doubling:
    def __init__(self, shard, order):
        self.current = shard[None]
        self.order = list(order)
        self.held = []

    def step(self):
        if not self.order:
            return
        bit = self.order.pop(0)
        current, held = self.current, self.held
        other = swap(current, bit)
        place = sum(1 for b in held if b > bit)
        shape = current.shape
        split = (1 << place, 1, shape[0] >> place) + shape[1:]
        mine, theirs = current.reshape(split), other.reshape(split)
        upper = my_bit(bit) == 1
        low = jnp.where(upper, theirs, mine)
        high = jnp.where(upper, mine, theirs)
        current = jnp.concatenate([low, high], axis=1).reshape((shape[0] * 2,) + shape[1:])
        held.append(bit)
        self.current = current

    def finish(self):
        while self.order:
            self.step()
        return self.current


def gather_rows(shard, order):
    return Doubling(shard, order).finish()


class Halving:
    def __init__(self, parts, order):
        self.current = parts
        self.order = list(order)
        self.left = sorted(order)

    def step(self):
        if not self.order:
            return
        bit = self.order.pop(0)
        place = sum(1 for b in self.left if b > bit)
        shape = self.current.shape
        view = self.current.reshape((1 << place, 2, shape[0] >> (place + 1)) + shape[1:])
        mine = my_bit(bit)
        sent = lax.dynamic_index_in_dim(view, 1 - mine, 1, keepdims=False)
        kept = lax.dynamic_index_in_dim(view, mine, 1, keepdims=False)
        got = swap(sent, bit)
        total = kept.astype(jnp.float32) + got.astype(jnp.float32)
        if self.order:
            total = total.astype(jnp.bfloat16)
        self.current = total.reshape((shape[0] // 2,) + shape[1:])
        self.left.remove(bit)

    def finish(self):
        while self.order:
            self.step()
        return self.current[0]


def advance(chains, *values):
    if not chains:
        return values if len(values) > 1 else values[0]
    held, values = lax.optimization_barrier((tuple(c.current for c in chains), values))
    for chain, current in zip(chains, held):
        chain.current = current
        chain.step()
    return values if len(values) > 1 else values[0]


def total_over(value, order):
    for bit in order:
        value = value + swap(value, bit)
    return value


def orders():
    bits = max(lax.axis_size("dp").bit_length() - 1, 0)
    far = list(range(3, bits))
    near_x = [bit for bit in (1, 2) if bit < bits]
    core = [0] if bits else []
    return core, near_x, far


def gather_order(flip):
    core, near, far = orders()
    return far + (near[::-1] if flip else near) + core


def scatter_order(flip):
    core, near, far = orders()
    return core + (near[::-1] if flip else near) + far[::-1]


def padded(height):
    return -(-height // 16) * 16


def spread(height, owners):
    pad = padded(height)
    row = lax.broadcasted_iota(jnp.int32, (height * owners, owners * pad), 0)
    column = lax.broadcasted_iota(jnp.int32, (height * owners, owners * pad), 1)
    inner = column % pad
    hit = (inner < height) & (row == column // pad * height + inner)
    return hit.astype(jnp.bfloat16)


def gather_padded(shard, chosen, flip):
    height = shard.shape[0]
    shard = jnp.pad(shard.astype(jnp.bfloat16), ((0, padded(height) - height), (0, 0)))
    full = gather_rows(shard, gather_order(flip))
    return matmul(chosen, full.reshape(-1, shard.shape[1])).astype(jnp.bfloat16)


def whole_rows(flat, width):
    return flat.shape[0] % width == 0


def gather_matrix(flat, width, flip):
    shard = flat.astype(jnp.bfloat16)
    if whole_rows(flat, width):
        shard = flat.reshape(-1, width).astype(jnp.bfloat16)
    return gather_rows(shard, gather_order(flip)).reshape(-1, width)


def scatter_matrix(grad, flip):
    owners = lax.axis_size("dp")
    grad = grad.astype(jnp.bfloat16)
    if grad.shape[0] % owners == 0:
        parts = grad.reshape(owners, grad.shape[0] // owners, grad.shape[1])
    else:
        parts = grad.reshape(owners, -1)
    return Halving(parts, scatter_order(flip))


def attend(query_rot, keys_rot, values, allowed, scale):
    scores = (
        jnp.einsum("bsgrd,btgd->bgrst", query_rot, keys_rot, preferred_element_type=jnp.float32)
        * scale
    )
    return jnp.where(allowed[:, None, None], scores, -1e30)


def body(
    tokens,
    position,
    cotangent,
    w_query,
    w_key,
    w_value,
    w_out,
    w_gate,
    w_up,
    w_down,
    gain_attn,
    gain_mlp,
):
    slots = SLOTS
    groups = H // KV
    kvw = KV * HD
    scale = 1.0 / math.sqrt(HD)
    rows = tokens.shape[0]
    blocks = rows // slots
    height = w_query.shape[0] // D
    aligned = whole_rows(w_query, D)
    if aligned:
        chosen = spread(height, lax.axis_size("dp"))
        joined = jnp.concatenate(
            [
                w_query.reshape(-1, D),
                w_key.reshape(-1, kvw),
                w_value.reshape(-1, kvw),
                w_out.reshape(-1, D),
            ],
            axis=1,
        )
        joined = gather_padded(joined, chosen, False)
        mat_qkv = joined[:, : D + 2 * kvw]
        mat_out = joined[:, D + 2 * kvw :]
    else:
        mat_qkv = jnp.concatenate(
            [
                gather_matrix(w_query, D, False),
                gather_matrix(w_key, kvw, False),
                gather_matrix(w_value, kvw, False),
            ],
            axis=1,
        )
        mat_out = gather_matrix(w_out, D, False)
    late = []
    if aligned:
        pad = padded(height) - height
        late = [
            Doubling(
                jnp.pad(flat.reshape(-1, FF).astype(jnp.bfloat16), ((0, pad), (0, 0))),
                gather_order(flip),
            )
            for flat, flip in ((w_gate, True), (w_up, False))
        ]
        late.append(Doubling(w_down.reshape(-1, D).astype(jnp.bfloat16), gather_order(True)))
        mat_qkv, mat_out = advance(late, mat_qkv, mat_out)

    def widen(value):
        return matmul(value, chosen).astype(jnp.bfloat16) if aligned else value

    allowed, placed, living = jax.vmap(block_mask)(position.reshape(blocks, slots))
    cosines, sines = rotary_tables(placed.reshape(-1), HD)
    living = living.reshape(-1)
    inputs = tokens.astype(jnp.float32)
    factor_one = lax.rsqrt(jnp.mean(inputs * inputs, axis=-1, keepdims=True) + EPS)
    normed = (inputs * factor_one * gain_attn).astype(jnp.bfloat16)
    qkv = matmul(normed, mat_qkv)
    qkv = advance(late, qkv)
    query = qkv[:, :D].reshape(rows, H, HD)
    keys = qkv[:, D : D + kvw].reshape(rows, KV, HD)
    values = qkv[:, D + kvw :].astype(jnp.bfloat16).reshape(blocks, slots, KV, HD)
    query_rot = (
        rotate(query, cosines, sines).astype(jnp.bfloat16).reshape(blocks, slots, KV, groups, HD)
    )
    keys_rot = rotate(keys, cosines, sines).astype(jnp.bfloat16).reshape(blocks, slots, KV, HD)
    query_rot, keys_rot = advance(late, query_rot, keys_rot)
    scores = attend(query_rot, keys_rot, values, allowed, scale)
    top = jnp.max(scores, axis=-1, keepdims=True)
    expd = jnp.exp(scores - top)
    total_exp = jnp.sum(expd, axis=-1, keepdims=True)
    probs = (expd / total_exp).astype(jnp.bfloat16)
    probs = advance(late, probs)
    mixed = jnp.einsum("bgrst,btgd->bsgrd", probs, values, preferred_element_type=jnp.float32)
    mixed = mixed.reshape(rows, D).astype(jnp.bfloat16)
    mixed = advance(late, mixed)
    resid = inputs + matmul(mixed, mat_out)
    if aligned:
        wide_gate, wide_up, wide_down = [c.finish() for c in late]
        mat_gate = matmul(chosen, wide_gate.reshape(-1, FF)).astype(jnp.bfloat16)
        mat_up = matmul(chosen, wide_up.reshape(-1, FF)).astype(jnp.bfloat16)
        mat_down = wide_down.reshape(-1, D)
    else:
        mat_gate = gather_matrix(w_gate, FF, True)
        mat_up = gather_matrix(w_up, FF, False)
        mat_down = gather_matrix(w_down, D, True)
    factor_two = lax.rsqrt(jnp.mean(resid * resid, axis=-1, keepdims=True) + EPS)
    normed_two = (resid * factor_two * gain_mlp).astype(jnp.bfloat16)
    wide_two = widen(normed_two)
    gate = matmul(normed_two, mat_gate)
    upper = matmul(normed_two, mat_up)
    sigma = jax.nn.sigmoid(gate)
    hidden = (gate * sigma * upper).astype(jnp.bfloat16)
    result = (resid + matmul(hidden, mat_down)).astype(jnp.bfloat16)

    grad_out = cotangent.astype(jnp.float32) * living[:, None].astype(jnp.float32)
    grad_out_b = grad_out.astype(jnp.bfloat16)
    down = scatter_matrix(left_contract(hidden, grad_out_b), False)
    grad_out_b = advance([down], grad_out_b)
    d_hidden = right_contract(grad_out_b, mat_down)
    d_upper = (d_hidden * gate * sigma).astype(jnp.bfloat16)
    d_gate = (d_hidden * upper * sigma * (1.0 + gate * (1.0 - sigma))).astype(jnp.bfloat16)
    d_upper, d_gate = advance([down], d_upper, d_gate)
    gated = scatter_matrix(left_contract(wide_two, d_gate), True)
    raised = scatter_matrix(left_contract(wide_two, d_upper), False)
    d_upper, d_gate = advance([gated, raised, down], d_upper, d_gate)
    d_normed_two = right_contract(d_gate, mat_gate) + right_contract(d_upper, mat_up)
    gain_two = jnp.sum(d_normed_two * resid * factor_two, axis=0)
    d_resid = grad_out + norm_back(d_normed_two, resid, factor_two, gain_mlp)
    d_attn = d_resid.astype(jnp.bfloat16)
    d_attn = advance([gated], d_attn)
    wout = scatter_matrix(left_contract(widen(mixed), d_attn), True)
    d_mixed = right_contract(d_attn, mat_out).astype(jnp.bfloat16)
    d_mixed = d_mixed.reshape(blocks, slots, KV, groups, HD)
    d_mixed = advance([wout, raised, down], d_mixed)
    d_probs = jnp.einsum("bsgrd,btgd->bgrst", d_mixed, values, preferred_element_type=jnp.float32)
    probs_back = expd / total_exp
    d_values = jnp.einsum("bgrst,bsgrd->btgd", probs, d_mixed, preferred_element_type=jnp.float32)
    d_values = d_values.reshape(rows, kvw).astype(jnp.bfloat16)
    d_scores = probs_back * (d_probs - jnp.sum(probs_back * d_probs, axis=-1, keepdims=True))
    d_scores = d_scores.astype(jnp.bfloat16)
    d_scores = advance([wout, gated, raised, down], d_scores)
    d_query_rot = (
        jnp.einsum("bgrst,btgd->bsgrd", d_scores, keys_rot, preferred_element_type=jnp.float32)
        * scale
    )
    d_keys_rot = (
        jnp.einsum("bgrst,bsgrd->btgd", d_scores, query_rot, preferred_element_type=jnp.float32)
        * scale
    )
    d_query_rot, d_keys_rot = advance([wout, gated, raised], d_query_rot, d_keys_rot)
    d_query = unrotate(d_query_rot.reshape(rows, H, HD), cosines, sines).reshape(rows, D)
    d_keys = unrotate(d_keys_rot.reshape(rows, KV, HD), cosines, sines).reshape(rows, kvw)
    d_qkv = jnp.concatenate(
        [d_query.astype(jnp.bfloat16), d_keys.astype(jnp.bfloat16), d_values], axis=1
    )
    d_qkv = advance([wout, gated, raised], d_qkv)
    grad_qkv = left_contract(widen(normed), d_qkv)
    if aligned:
        joint = scatter_matrix(grad_qkv, False)
        d_qkv = advance([joint, wout], d_qkv)
    d_normed = right_contract(d_qkv, mat_qkv)
    gain_one = jnp.sum(d_normed * inputs * factor_one, axis=0)
    d_inputs = (d_resid + norm_back(d_normed, inputs, factor_one, gain_attn)).astype(jnp.bfloat16)
    gains = total_over(jnp.stack([gain_one, gain_two]), scatter_order(True))
    if aligned:
        sum_qkv = joint.finish()[:height]
        sum_query = sum_qkv[:, :D]
        sum_key = sum_qkv[:, D : D + kvw]
        sum_value = sum_qkv[:, D + kvw :]
        sum_wout, sum_gate, sum_up = [c.finish()[:height] for c in (wout, gated, raised)]
    else:
        sum_query = scatter_matrix(grad_qkv[:, :D], False).finish()
        sum_key = scatter_matrix(grad_qkv[:, D : D + kvw], False).finish()
        sum_value = scatter_matrix(grad_qkv[:, D + kvw :], False).finish()
        sum_wout, sum_gate, sum_up = wout.finish(), gated.finish(), raised.finish()
    sum_down = down.finish()
    return (
        result,
        d_inputs,
        sum_query.reshape(-1),
        sum_key.reshape(-1),
        sum_value.reshape(-1),
        sum_wout.reshape(-1),
        sum_gate.reshape(-1),
        sum_up.reshape(-1),
        sum_down.reshape(-1),
        gains[0],
        gains[1],
    )


def solution(mesh):
    placed = (
        P("dp", None),
        P("dp"),
        P("dp", None),
        P("dp"),
        P("dp"),
        P("dp"),
        P("dp"),
        P("dp"),
        P("dp"),
        P("dp"),
        P(),
        P(),
    )
    return jax.shard_map(
        body,
        mesh=mesh,
        in_specs=placed,
        out_specs=(
            P("dp", None),
            P("dp", None),
            P("dp"),
            P("dp"),
            P("dp"),
            P("dp"),
            P("dp"),
            P("dp"),
            P("dp"),
            P(),
            P(),
        ),
        check_vma=False,
    )
```
